32 devices in a mesh: parts: 2 (over x), inst: 4 (over y, core), tp: 4 (over z).
Axes of the slice: x: 2, y: 2, z: 4, core: 2. Of those that a mesh axis runs over, the one named last changes fastest.
Arguments:
- queries: bfloat16 [4096, 8192], P(('parts', 'inst'), 'tp'), parts along dimension 0, may hold values from -8 to 8
- keys: bfloat16 [4096, 1024], P(('parts', 'inst'), 'tp'), parts along dimension 0, may hold values from -6 to 6
- values: bfloat16 [4096, 1024], P(('parts', 'inst'), 'tp'), parts along dimension 0, may hold values from -6 to 6
- prefix_pool_keys: bfloat16 [128, 64, 1024], P(('parts', 'inst'), None, 'tp'), parts along dimension 0, may hold values from -8 to 8
- prefix_pool_values: bfloat16 [128, 64, 1024], P(('parts', 'inst'), None, 'tp'), parts along dimension 0, may hold values from -6 to 6
- lengths: int32 [64], P(('parts', 'inst')), parts along dimension 0, may hold values from 1 to 64, 1536 in all
- targets: int32 [64, 1], P(('parts', 'inst')), parts along dimension 0, may hold values from 0 to 3; in each aligned block of 8 rows (0 to 7, 8 to 15, ...) at most 2 rows name the same one
- prefix_ids: int32 [64, 8], P(('parts', 'inst')), parts along dimension 0, may hold values from 0 to 15
- owners: int32 [64, 1], P(('parts', 'inst')), parts along dimension 0, may hold values from 0 to 3; in each aligned block of 8 rows (0 to 7, 8 to 15, ...) at most 2 rows name the same one
- out_weight: bfloat16 [8192, 4096], P('tp'), may hold values from -0.0625 to 0.0625
Outputs:
- projected: bfloat16 [64, 64, 4096], P(('parts', 'inst'), None, 'tp'), parts along dimension 0
- pages: bfloat16 [64, 2, 64, 1024], P(('parts', 'inst'), None, None, 'tp'), parts along dimension 0
- page_head_scales: bfloat16 [64, 2, 8], P(('parts', 'inst'), None, 'tp'), parts along dimension 0
The draws below stay inside these ranges and needn't reach their ends.
There are 2 independent parts, one for each index of `parts`. The reference program is written for one: setup_inputs(seed, part) draws one part's arguments, and reference() takes and returns one part's arrays. A program takes and returns all parts, laid end to end along the dimension named above; an argument that names none is the same for every part. Nothing has to cross between parts.
Inputs may be any that keep to these rules, and one draw needn't show every extreme that they name: `targets`: no instance sends more than 2 of its blocks to one instance, and some instance receives exactly 2 from one instance. `owners`: no instance sends more than 2 of its pages to one instance, and some instance receives exactly 2 from one instance.
All inputs are finite; a program needn't handle non-finite values. No bound on the sum of `lengths` on one device may be relied on, other than what follows from the above.
Results may differ from the reference program's by a relative error of at most 0.0095.
Values may be sent and summed in bfloat16 or wider, within the bound.
A program may use at most 128 MiB of HBM per device.

```python
import math
import jax
import jax.numpy as jnp
import numpy as np
from jax import lax

QUERY_HEADS = 64
KEY_VALUE_HEADS = 8
HEAD_SIZE = 128
DOUT = 4096
BLOCK_TOKENS = 64
NB = 8
ATTENDED_BLOCKS = 8
LOCAL_PREFIXES = 16
CAP = 2
PROMPT_BLOCKS = 32
TOKEN_POSITIONS = 2048
PREFIX_BLOCKS = 64
RECEIVER_SLOTS = 32
N_INST = 4
N_TP = 4


def draw_queries(key, part):
    key = jax.random.fold_in(key, 5)
    rows = NB * N_INST * BLOCK_TOKENS
    base = jnp.clip(jax.random.normal(key, (rows, QUERY_HEADS * HEAD_SIZE), jnp.float32), -6.0, 6.0)
    return base.astype(jnp.bfloat16)


def draw_prefix_pool_keys(key, part):
    key = jax.random.fold_in(key, 9)
    array_shape = (LOCAL_PREFIXES * N_INST, BLOCK_TOKENS, KEY_VALUE_HEADS * HEAD_SIZE)
    base = jnp.clip(jax.random.normal(key, array_shape, jnp.float32), -6.0, 6.0)
    return base.astype(jnp.bfloat16)


def touch_ends(values, key, low, top_value):
    spot = [jax.random.randint(jax.random.fold_in(key, axis), (), 0, length) for axis, length in enumerate(values.shape)]
    main_axis = values.shape.index(max(values.shape))
    next_to = spot[:main_axis] + [(spot[main_axis] + 1) % values.shape[main_axis]] + spot[main_axis + 1:]
    return values.at[tuple(spot)].set(low).at[tuple(next_to)].set(top_value)


def level_of(stream_key, dims, cuts, least, largest):
    factor_of = 1.0
    for position, blocks in cuts:
        steps = jax.random.uniform(jax.random.fold_in(jax.random.fold_in(stream_key, 6), position), (blocks,), jnp.float32, least / len(cuts), largest / len(cuts))
        factor_of = factor_of * jnp.repeat(jnp.exp(steps), dims[position] // blocks).reshape((-1,) + (1,) * (len(dims) - 1 - position))
    return factor_of


def length_profile(count, total, reach, skew):
    weights = [(1 << 20) // math.isqrt(rank ** skew) + 1 for rank in range(2, count + 1)]
    spare, given = total - reach - (count - 1), [1] * (count - 1)
    while spare > 0:
        movable = [i for i in range(count - 1) if given[i] < reach]
        pool, budget = sum([weights[i] for i in movable]), spare
        for i in movable:
            addition = min(reach - given[i], max(1, budget * weights[i] // pool), spare)
            given[i] = given[i] + addition
            spare = spare - addition
    return np.array([reach] + given)


def uneven_parts(stream_key, amount, total, reach, skew):
    if amount == 2:
        one = jax.random.randint(stream_key, (), max(1, total - reach), min(reach, total - 1) + 1)
        return jnp.stack([one, total - one])
    tallies = jnp.asarray(length_profile(amount, total, reach, skew), jnp.int32)
    couples = (amount - 1) // 2
    source_of, receiver = tallies[1:1 + 2 * couples:2], tallies[2:2 + 2 * couples:2]
    room = jnp.minimum(source_of - 1, reach - receiver)
    shifted = jax.random.randint(jax.random.fold_in(stream_key, 1), (couples,), 0, 1 << 20) % (room + 1)
    tallies = tallies.at[1:1 + 2 * couples:2].set(source_of - shifted).at[2:2 + 2 * couples:2].set(receiver + shifted)
    return tallies[jax.random.permutation(jax.random.fold_in(stream_key, 2), amount)]


def routed_block(own_key, own, number, rows, number_of, top, limit, slope):
    sequence = jax.random.permutation(own_key, number_of)
    packed, usual = load_shares(number_of, rows * top, limit, slope, True), load_shares(number_of, rows * top, limit, slope, False)
    places = jnp.arange(number_of)

    def named(tallies, offset_by):
        used = int((tallies > 0).sum())
        fixed = max(1, used // 4)
        moved = fixed + (places - fixed + offset_by * (used - fixed)) % max(1, number_of - fixed)
        return jnp.zeros((number_of,), jnp.int32).at[sequence[jnp.where(places < fixed, places, moved)]].set(jnp.asarray(tallies, jnp.int32))

    tallies = jnp.where(number % 4 == 0, named(packed, number // 4), named(usual, number - number // 4 - 1))
    mixed = jax.random.permutation(jax.random.fold_in(own, 3), number_of)
    donor, receiver = mixed[0:number_of // 2 * 2:2], mixed[1:number_of // 2 * 2:2]
    room = jnp.minimum(tallies[donor] - 1, limit - tallies[receiver]) // 2
    room = jnp.where((donor == sequence[0]) | (receiver == sequence[0]) | (tallies[receiver] == 0), 0, jnp.maximum(room, 0))
    moved = jax.random.randint(jax.random.fold_in(own, 4), (number_of // 2,), 0, 1 << 20) % (room + 1)
    tallies = tallies.at[donor].add(-moved).at[receiver].add(moved)
    items = jnp.searchsorted(jnp.cumsum(tallies), jnp.arange(rows * top), side="right").astype(jnp.int32)
    table = items.reshape(top, rows).T
    table = table[jax.random.permutation(jax.random.fold_in(own, 1), rows)]
    offset_by = jax.random.randint(jax.random.fold_in(own, 2), (rows, 1), 0, top)
    return jnp.take_along_axis(table, (jnp.arange(top)[None, :] + offset_by) % top, axis=1)


def load_shares(number_of, total, limit, skew, full):
    loads = [(1 << 20) // math.isqrt(standing ** skew) + 1 for standing in range(1, number_of + 1)]
    largest = limit if full else min(limit, max(-(-total // number_of), total * loads[0] // sum(loads)))
    least = 1 if total - largest >= number_of - 1 else 0
    counts, spare = [largest] + [least] * (number_of - 1), total - largest - least * (number_of - 1)
    while spare > 0:
        free = [i for i in range(1, number_of) if counts[i] < largest] or [i for i in range(1, number_of) if counts[i] < limit]
        whole, budget = sum([loads[i] for i in free]), spare
        for i in free:
            addition = min(limit - counts[i], max(1, budget * loads[i] // whole), spare)
            counts[i] = counts[i] + addition
            spare = spare - addition
    return np.array(counts)


def bell_draw(rng, extent, width, most, split=(), kind=jnp.bfloat16):
    entries = width * jax.random.normal(rng, extent, jnp.float32)
    if split:
        entries = entries * level_of(rng, extent, split, -0.22, 0.18)
    return jnp.clip(entries, -most, most).astype(kind)


def setup_inputs(seed: int = 0, part: int = 0) -> dict:
    key_list = jax.random.split(jax.random.key(seed), 11)
    part_splits = jax.random.split(jax.random.fold_in(key_list[10], part), 11)
    queries = draw_queries(jax.random.fold_in(jax.random.fold_in(key_list[10], part), 71), part)
    keys = bell_draw(part_splits[1], (TOKEN_POSITIONS, KEY_VALUE_HEADS * HEAD_SIZE), 1.0, 6.0, ((0, 4), (1, 4)))
    values = bell_draw(part_splits[2], (TOKEN_POSITIONS, KEY_VALUE_HEADS * HEAD_SIZE), 1.0, 6.0, ((0, 4), (1, 4)))
    prefix_pool_keys = draw_prefix_pool_keys(jax.random.fold_in(jax.random.fold_in(key_list[10], part), 71), part)
    prefix_pool_values = bell_draw(part_splits[4], (PREFIX_BLOCKS, BLOCK_TOKENS, KEY_VALUE_HEADS * HEAD_SIZE), 1.0, 6.0, ((0, 4), (2, 4)))
    lengths = uneven_parts(part_splits[5], PROMPT_BLOCKS, PROMPT_BLOCKS * BLOCK_TOKENS * 3 // 4, BLOCK_TOKENS, 2).astype(jnp.int32)
    targets_keys = jax.random.split(jax.random.fold_in(part_splits[6], 1), PROMPT_BLOCKS // NB)
    targets_turns = jax.random.permutation(jax.random.fold_in(part_splits[6], 3), PROMPT_BLOCKS // NB)
    targets = jax.vmap(lambda own, number: routed_block(jax.random.fold_in(part_splits[6], 2), own, number, NB, N_INST, 1, CAP, 2))(targets_keys, targets_turns).reshape((PROMPT_BLOCKS, 1))
    prefix_ids = touch_ends(jax.random.randint(part_splits[7], (PROMPT_BLOCKS, ATTENDED_BLOCKS), 0, LOCAL_PREFIXES), jax.random.fold_in(part_splits[7], 1), 0, LOCAL_PREFIXES - 1).astype(jnp.int32)
    owners_keys = jax.random.split(jax.random.fold_in(part_splits[8], 1), PROMPT_BLOCKS // NB)
    owners_turns = jax.random.permutation(jax.random.fold_in(part_splits[8], 3), PROMPT_BLOCKS // NB)
    owners = jax.vmap(lambda own, number: routed_block(jax.random.fold_in(part_splits[8], 2), own, number, NB, N_INST, 1, CAP, 1))(owners_keys, owners_turns).reshape((PROMPT_BLOCKS, 1))
    out_weight = bell_draw(key_list[9], (QUERY_HEADS * HEAD_SIZE, DOUT), (QUERY_HEADS * HEAD_SIZE) ** -0.5, 0.0625, ((0, 4),))
    return {"queries": queries, "keys": keys, "values": values, "prefix_pool_keys": prefix_pool_keys, "prefix_pool_values": prefix_pool_values, "lengths": lengths, "targets": targets, "prefix_ids": prefix_ids, "owners": owners, "out_weight": out_weight}


def hadamard_table(size):
    index = jnp.arange(size, dtype=jnp.int32)
    common = jnp.bitwise_and(index[:, None], index[None, :])
    parity = jnp.zeros((size, size), jnp.int32)
    for bit_number in range(size.bit_length() - 1):
        parity = parity + jnp.bitwise_and(jnp.right_shift(common, bit_number), 1)
    return jnp.where(jnp.bitwise_and(parity, 1) == 0, 1.0, -1.0).astype(jnp.bfloat16)

def slot_of(route):
    choices_hot = (route.reshape(N_INST, NB)[:, :, None] == jnp.arange(N_INST, dtype=jnp.int32)[None, None, :]).astype(jnp.int32)
    before = jnp.cumsum(choices_hot, axis=1) - choices_hot
    rank = lax.optimization_barrier(jnp.sum(before * choices_hot, axis=2)).reshape(-1)
    home = jnp.arange(N_INST * NB, dtype=jnp.int32) // NB
    return route * (N_INST * CAP) + home * CAP + rank

def attend(query_block, gathered_keys, gathered_values, length):
    head_group = QUERY_HEADS // KEY_VALUE_HEADS
    query_rows = query_block.astype(jnp.float32).reshape(BLOCK_TOKENS, KEY_VALUE_HEADS, head_group, HEAD_SIZE)
    key_row_list = gathered_keys.astype(jnp.float32).reshape(-1, KEY_VALUE_HEADS, HEAD_SIZE)
    value_row_list = gathered_values.astype(jnp.float32).reshape(-1, KEY_VALUE_HEADS, HEAD_SIZE)
    scores = jnp.einsum('tkgd,skd->kgts', query_rows, key_row_list) / math.sqrt(HEAD_SIZE)
    ctx_len = key_row_list.shape[0]
    prefix_len = ctx_len - BLOCK_TOKENS
    qpos = jnp.arange(BLOCK_TOKENS, dtype=jnp.int32)[:, None]
    kpos = jnp.arange(ctx_len, dtype=jnp.int32)[None, :]
    own = kpos - prefix_len
    allowed = (kpos < prefix_len) | (own <= qpos) & (own < length)
    top = lax.optimization_barrier(jnp.max(jnp.where(allowed, scores, jnp.float32(-1e+30)), axis=-1, keepdims=True))
    expo = jnp.where(allowed, jnp.exp(scores - top), jnp.float32(0.0))
    total = lax.optimization_barrier(jnp.sum(expo, axis=-1, keepdims=True))
    weights = expo.astype(jnp.bfloat16).astype(jnp.float32)
    mixed = jnp.einsum('kgts,skd->kgtd', weights, value_row_list) / total
    mixed = mixed.transpose(2, 0, 1, 3).reshape(BLOCK_TOKENS, QUERY_HEADS * HEAD_SIZE)
    live = jnp.arange(BLOCK_TOKENS, dtype=jnp.int32)[:, None] < length
    return jnp.where(live, mixed, jnp.float32(0.0)).astype(jnp.bfloat16)

def reference(queries, keys, values, prefix_pool_keys, prefix_pool_values, lengths, targets, prefix_ids, owners, out_weight):

    def one_block(index):
        home = index // NB
        block_ids = (home * LOCAL_PREFIXES + prefix_ids[index]).astype(jnp.int32)
        local_keys = lax.dynamic_slice_in_dim(keys, (index * BLOCK_TOKENS).astype(jnp.int32), BLOCK_TOKENS, 0)
        local_values = lax.dynamic_slice_in_dim(values, (index * BLOCK_TOKENS).astype(jnp.int32), BLOCK_TOKENS, 0)
        context_keys = jnp.concatenate([prefix_pool_keys[block_ids].reshape(ATTENDED_BLOCKS * BLOCK_TOKENS, KEY_VALUE_HEADS * HEAD_SIZE), local_keys], axis=0)
        context_values = jnp.concatenate([prefix_pool_values[block_ids].reshape(ATTENDED_BLOCKS * BLOCK_TOKENS, KEY_VALUE_HEADS * HEAD_SIZE), local_values], axis=0)
        query_block = lax.dynamic_slice_in_dim(queries, (index * BLOCK_TOKENS).astype(jnp.int32), BLOCK_TOKENS, 0)
        return attend(query_block, context_keys, context_values, lengths[index])
    attn = lax.map(one_block, jnp.arange(PROMPT_BLOCKS, dtype=jnp.int32)).reshape(PROMPT_BLOCKS * BLOCK_TOKENS, QUERY_HEADS * HEAD_SIZE)
    per = QUERY_HEADS * HEAD_SIZE // N_TP
    summed = jnp.zeros((PROMPT_BLOCKS * BLOCK_TOKENS, DOUT), jnp.float32)
    for group_index in range(N_TP):
        term = jnp.dot(attn[:, group_index * per:(group_index + 1) * per], out_weight[group_index * per:(group_index + 1) * per], preferred_element_type=jnp.float32).astype(jnp.bfloat16)
        summed = summed + lax.optimization_barrier(term).astype(jnp.float32)
    result = summed.astype(jnp.bfloat16).reshape(PROMPT_BLOCKS, BLOCK_TOKENS, DOUT)
    run_slot = slot_of(targets[:, 0])
    projected = jnp.zeros((RECEIVER_SLOTS, BLOCK_TOKENS, DOUT), jnp.bfloat16).at[run_slot].set(result)
    live = jnp.arange(BLOCK_TOKENS, dtype=jnp.int32)[None, :] < lengths[:, None]
    stacked_pages = jnp.stack([keys.reshape(PROMPT_BLOCKS, BLOCK_TOKENS, KEY_VALUE_HEADS * HEAD_SIZE), values.reshape(PROMPT_BLOCKS, BLOCK_TOKENS, KEY_VALUE_HEADS * HEAD_SIZE)], axis=1)
    stacked_pages = jnp.where(live[:, None, :, None], stacked_pages, jnp.zeros((), jnp.bfloat16))
    rotation_matrix = jnp.dot(stacked_pages.reshape(-1, HEAD_SIZE), hadamard_table(HEAD_SIZE), preferred_element_type=jnp.float32) / math.sqrt(HEAD_SIZE)
    rotation_matrix = rotation_matrix.reshape(PROMPT_BLOCKS, 2, BLOCK_TOKENS, KEY_VALUE_HEADS, HEAD_SIZE)
    peak = lax.optimization_barrier(jnp.max(jnp.abs(rotation_matrix), axis=(2, 4)))
    scale_factor = ((peak + 1e-06) / 8.0).astype(jnp.bfloat16)
    quantized_page = (rotation_matrix / lax.optimization_barrier(scale_factor).astype(jnp.float32)[:, :, None, :, None]).astype(jnp.bfloat16)
    quantized_page = quantized_page.reshape(PROMPT_BLOCKS, 2, BLOCK_TOKENS, KEY_VALUE_HEADS * HEAD_SIZE)
    page_target_slot = slot_of(owners[:, 0])
    pages = jnp.zeros((RECEIVER_SLOTS, 2, BLOCK_TOKENS, KEY_VALUE_HEADS * HEAD_SIZE), jnp.bfloat16).at[page_target_slot].set(quantized_page)
    page_head_scales = jnp.zeros((RECEIVER_SLOTS, 2, KEY_VALUE_HEADS), jnp.bfloat16).at[page_target_slot].set(scale_factor)
    return (projected, pages, page_head_scales)
```

```python
import functools
import math

import jax
import jax.numpy as jnp
from jax import lax
from jax.experimental import pallas as pl
from jax.experimental.pallas import tpu as pltpu
from jax.sharding import PartitionSpec as P

HEAD_SIZE = 128
MESH = pl.DeviceIdType.MESH


def hadamard_table(size):
    row = lax.broadcasted_iota(jnp.int32, (size, size), 0)
    col = lax.broadcasted_iota(jnp.int32, (size, size), 1)
    common = jnp.bitwise_and(row, col)
    parity = jnp.zeros((size, size), jnp.int32)
    for bit_number in range(size.bit_length() - 1):
        parity = parity + jnp.bitwise_and(jnp.right_shift(common, bit_number), 1)
    return jnp.where(jnp.bitwise_and(parity, 1) == 0, 1.0, -1.0).astype(jnp.bfloat16)


def block_of(route_ref, blocks, group, rank):
    seen, found, valid = jnp.int32(0), jnp.int32(0), jnp.int32(0)
    for b in range(blocks):
        hit = (route_ref[b, 0] == group).astype(jnp.int32)
        take = hit * (seen == rank).astype(jnp.int32)
        found = found + take * b
        valid = valid + take
        seen = seen + hit
    return found, valid


def attend(q_ref, k_ref, v_ref, pk_ref, pv_ref, ids_ref, block, length, attn_ref, row):
    block_len = q_ref.shape[1]
    kv_heads = k_ref.shape[2] // HEAD_SIZE
    group = q_ref.shape[2] // k_ref.shape[2]
    attended = ids_ref.shape[1]
    rate = math.log2(math.e) / math.sqrt(HEAD_SIZE)
    rows = group * block_len
    nt = (((1,), (1,)), ((), ()))
    token = lax.rem(lax.broadcasted_iota(jnp.int32, (rows, block_len), 0), block_len)
    place = lax.broadcasted_iota(jnp.int32, (rows, block_len), 1)
    allowed = (place <= token) & (place < length)
    live = lax.broadcasted_iota(jnp.int32, (block_len, HEAD_SIZE), 0) < length
    ids = [ids_ref[block, a] for a in range(attended)]
    for h in range(kv_heads):
        lanes = slice(h * HEAD_SIZE, (h + 1) * HEAD_SIZE)
        base = h * group * HEAD_SIZE
        q = jnp.concatenate(
            [q_ref[block, :, base + g * HEAD_SIZE : base + (g + 1) * HEAD_SIZE] for g in range(group)], axis=0
        )
        prefix_k = jnp.concatenate([pk_ref[i, :, lanes] for i in ids], axis=0)
        prefix_v = jnp.concatenate([pv_ref[i, :, lanes] for i in ids], axis=0)
        s0 = lax.dot_general(q, prefix_k, nt, preferred_element_type=jnp.float32)
        s1 = lax.dot_general(q, k_ref[block, :, lanes], nt, preferred_element_type=jnp.float32)
        s1 = jnp.where(allowed, s1, jnp.float32(-1e30))
        top = jnp.maximum(
            jnp.max(s0, axis=1, keepdims=True), jnp.max(s1, axis=1, keepdims=True)
        )
        p0 = jnp.exp2((s0 - top) * rate).astype(jnp.bfloat16)
        p1 = jnp.where(allowed, jnp.exp2((s1 - top) * rate), 0.0).astype(jnp.bfloat16)
        v0 = jnp.concatenate([prefix_v, jnp.ones_like(prefix_v)], axis=1)
        own_v = v_ref[block, :, lanes]
        v1 = jnp.concatenate([own_v, jnp.ones_like(own_v)], axis=1)
        mixed = jnp.dot(p0, v0, preferred_element_type=jnp.float32) + jnp.dot(
            p1, v1, preferred_element_type=jnp.float32
        )
        mixed = mixed[:, :HEAD_SIZE] / mixed[:, HEAD_SIZE:]
        for g in range(group):
            part = mixed[g * block_len : (g + 1) * block_len]
            attn_ref[row, :, base + g * HEAD_SIZE : base + (g + 1) * HEAD_SIZE] = jnp.where(
                live, part, 0.0
            ).astype(jnp.bfloat16)


def make_page(k_ref, v_ref, block, length, valid, table, page_ref, scale_ref, at, row):
    block_len = k_ref.shape[1]
    kv_heads = k_ref.shape[2] // HEAD_SIZE
    live = lax.broadcasted_iota(jnp.int32, (block_len, HEAD_SIZE), 0) < length
    tile_row = lax.broadcasted_iota(jnp.int32, (8, HEAD_SIZE), 0)
    tile_lane = lax.broadcasted_iota(jnp.int32, (8, HEAD_SIZE), 1)
    tile = jnp.zeros((8, HEAD_SIZE), jnp.float32)
    for which, ref in enumerate((k_ref, v_ref)):
        for h in range(kv_heads):
            lanes = slice(h * HEAD_SIZE, (h + 1) * HEAD_SIZE)
            data = jnp.where(live, ref[block, :, lanes].astype(jnp.float32), 0.0).astype(jnp.bfloat16)
            rot = jnp.dot(data, table, preferred_element_type=jnp.float32) / math.sqrt(HEAD_SIZE)
            peak = jnp.max(jnp.max(jnp.abs(rot), axis=1, keepdims=True), axis=0, keepdims=True)
            scale = ((peak + 1e-06) / 8.0).astype(jnp.bfloat16).astype(jnp.float32)
            page_ref[at, row, which * block_len : (which + 1) * block_len, lanes] = (
                rot / scale
            ).astype(jnp.bfloat16)
            tile = jnp.where((tile_row == which) & (tile_lane == h), scale, tile)
    scale_ref[at, row] = tile * valid.astype(jnp.float32)


def kernel(
    groups, tps, capacity,
    q_ref, k_ref, v_ref, pk_ref, pv_ref, len_ref, tgt_ref, ids_ref, own_ref, w_ref,
    proj_ref, page_ref, scale_ref,
    w_buf, attn, send, recv, final, page_buf, scale_buf,
    w_sem, send_sem, recv_sem, ship_send, ship_recv, page_send, page_recv, scale_send, scale_recv, local_sem,
):
    part, inst, me = lax.axis_index("parts"), lax.axis_index("inst"), lax.axis_index("tp")
    blocks, block_len = q_ref.shape[0], q_ref.shape[1]
    share = w_buf.shape[2]
    last = tps - 1
    far = last - me

    def dest_at(p):
        right = p < far
        return jnp.where(right, last - p, jnp.where(p < last, p - far, me))

    def w_copy(p):
        j = dest_at(p)
        columns = pl.ds(pl.multiple_of(j * share, share), share)
        return pltpu.make_async_copy(w_ref.at[:, columns], w_buf.at[j], w_sem.at[p])

    for p in range(tps):
        w_copy(p).start()

    barrier = pltpu.get_barrier_semaphore()
    for d in range(1, groups):
        other = lax.rem(inst + d, groups)
        pl.semaphore_signal(barrier, inc=1, device_id=(part, other, me), device_id_type=MESH)

    @pl.when(me > 0)
    def _():
        pl.semaphore_signal(barrier, inc=1, device_id=(part, inst, me - 1), device_id_type=MESH)

    @pl.when(me < last)
    def _():
        pl.semaphore_signal(barrier, inc=1, device_id=(part, inst, me + 1), device_id_type=MESH)

    def target(i):
        return lax.rem(inst + 1 + i, groups)

    def source(i):
        return lax.rem(inst + groups - 1 - i, groups)

    table = hadamard_table(HEAD_SIZE)

    def page_step(n, carry):
        i, r = n // capacity, n % capacity
        b, valid = block_of(own_ref, blocks, target(i), r)
        length = len_ref[b] * valid
        make_page(k_ref, v_ref, b, length, valid, table, page_buf, scale_buf, i, r)
        return carry

    lax.fori_loop(0, groups * capacity, page_step, 0)

    neighbours = (me > 0).astype(jnp.int32) + (me < last).astype(jnp.int32)
    pl.semaphore_wait(barrier, groups - 1 + neighbours)

    def page_copies(i, home):
        to = (part, target(i), me)
        slots = pl.ds(home * capacity, capacity)
        return (
            pltpu.make_async_remote_copy(
                src_ref=page_buf.at[i], dst_ref=page_ref.at[slots],
                send_sem=page_send.at[i], recv_sem=page_recv.at[i], device_id=to, device_id_type=MESH,
            ),
            pltpu.make_async_remote_copy(
                src_ref=scale_buf.at[i], dst_ref=scale_ref.at[slots],
                send_sem=scale_send.at[i], recv_sem=scale_recv.at[i], device_id=to, device_id_type=MESH,
            ),
        )

    def ship_copy(i, home):
        rows = pl.ds(pl.multiple_of(home * capacity * block_len, capacity * block_len), capacity * block_len)
        return pltpu.make_async_remote_copy(
            src_ref=final.at[i], dst_ref=proj_ref.at[rows],
            send_sem=ship_send.at[i], recv_sem=ship_recv.at[i],
            device_id=(part, target(i), me), device_id_type=MESH,
        )

    own = groups - 1
    own_slots = pl.ds(inst * capacity, capacity)
    own_rows = pl.ds(pl.multiple_of(inst * capacity * block_len, capacity * block_len), capacity * block_len)
    local_copies = (
        pltpu.make_async_copy(page_buf.at[own], page_ref.at[own_slots], local_sem.at[0]),
        pltpu.make_async_copy(scale_buf.at[own], scale_ref.at[own_slots], local_sem.at[1]),
        pltpu.make_async_copy(final.at[own], proj_ref.at[own_rows], local_sem.at[2]),
    )
    for i in range(groups - 1):
        for copy in page_copies(i, inst):
            copy.start()
    local_copies[0].start()
    local_copies[1].start()

    def sum_copy(i, j):
        towards = jnp.where(j > me, me + 1, me - 1)
        slot = jnp.where((j < me) & (j == towards), tps, j)
        return pltpu.make_async_remote_copy(
            src_ref=send.at[i, j], dst_ref=recv.at[i, slot],
            send_sem=send_sem.at[i, j], recv_sem=recv_sem.at[i, slot],
            device_id=(part, inst, towards), device_id_type=MESH,
        )

    def arrived(i, slot):
        pltpu.make_async_copy(recv.at[i, slot], recv.at[i, slot], recv_sem.at[i, slot]).wait()

    def has_upstream(j):
        return ((j > me) & (me > 0)) | ((j < me) & (me < last))

    def compute(i):
        def one(r, carry):
            b, valid = block_of(tgt_ref, blocks, target(i), r)
            attend(q_ref, k_ref, v_ref, pk_ref, pv_ref, ids_ref, b, len_ref[b] * valid, attn, r)
            return carry

        lax.fori_loop(0, capacity, one, 0)
        wide = 256 if share % 256 == 0 else share

        def term(p, carry):
            j = dest_at(p)

            @pl.when(i == 0)
            def _():
                w_copy(p).wait()

            def columns(c, inner):
                lanes = pl.ds(pl.multiple_of(c * wide, wide), wide)
                rows = attn[...].reshape(capacity * block_len, attn.shape[2])
                send[i, j, :, lanes] = jnp.dot(
                    rows, w_buf[j, :, lanes], preferred_element_type=jnp.float32
                ).astype(jnp.bfloat16)
                return inner

            lax.fori_loop(0, share // wide, columns, 0)

            @pl.when((p < last) & jnp.logical_not(has_upstream(j)))
            def _():
                sum_copy(i, j).start()

            return carry

        lax.fori_loop(0, tps, term, 0)

    def forward(i):
        def one(p, carry):
            j = dest_at(p)

            @pl.when(has_upstream(j))
            def _():
                arrived(i, j)
                send[i, j] = (send[i, j].astype(jnp.float32) + recv[i, j].astype(jnp.float32)).astype(jnp.bfloat16)
                sum_copy(i, j).start()

            return carry

        lax.fori_loop(0, last, one, 0)

    def finish(i):
        final[i] = send[i, me]

        @pl.when((me > 0) & (me < last))
        def _():
            arrived(i, me)
            arrived(i, tps)
            final[i] = (
                send[i, me].astype(jnp.float32)
                + recv[i, me].astype(jnp.float32)
                + recv[i, tps].astype(jnp.float32)
            ).astype(jnp.bfloat16)

        @pl.when((me > 0) & (me == last))
        def _():
            arrived(i, me)
            final[i] = (send[i, me].astype(jnp.float32) + recv[i, me].astype(jnp.float32)).astype(jnp.bfloat16)

        @pl.when((me == 0) & (me < last))
        def _():
            arrived(i, tps)
            final[i] = (send[i, me].astype(jnp.float32) + recv[i, tps].astype(jnp.float32)).astype(jnp.bfloat16)

        @pl.when(i < own)
        def _():
            ship_copy(i, inst).start()

    def step(i, carry):
        @pl.when(i < groups)
        def _():
            compute(i)

        @pl.when(i > 0)
        def _():
            forward(i - 1)

        @pl.when(i > 1)
        def _():
            finish(i - 2)

        return carry

    lax.fori_loop(0, groups + 1, step, 0)
    finish(own)
    local_copies[2].start()

    def drain(i, carry):
        def one(p, inner):
            sum_copy(i, dest_at(p)).wait_send()
            return inner

        return lax.fori_loop(0, last, one, carry)

    lax.fori_loop(0, groups, drain, 0)
    for i in range(groups - 1):
        ship_copy(i, inst).wait_send()
        for copy in page_copies(i, inst):
            copy.wait_send()
        ship_copy(i, source(i)).wait_recv()
        for copy in page_copies(i, source(i)):
            copy.wait_recv()
    for copy in local_copies:
        copy.wait()


def on_device(
    queries, keys, values, prefix_pool_keys, prefix_pool_values,
    lengths, targets, prefix_ids, owners, out_weight,
):
    groups, tps = lax.axis_size("inst"), lax.axis_size("tp")
    blocks, block_len = lengths.shape[0], prefix_pool_keys.shape[1]
    kv_width = keys.shape[1]
    kv_heads = kv_width // HEAD_SIZE
    capacity = max(1, (blocks + groups - 1) // groups)
    depth, dout = out_weight.shape
    share = dout // tps
    slots = groups * capacity
    rows = capacity * block_len
    vmem = pl.BlockSpec(memory_space=pltpu.VMEM)
    smem = pl.BlockSpec(memory_space=pltpu.SMEM)
    anywhere = pl.BlockSpec(memory_space=pl.ANY)
    dma = pltpu.SemaphoreType.DMA
    bf16 = jnp.bfloat16
    proj, pages, scales = pl.pallas_call(
        functools.partial(kernel, groups, tps, capacity),
        out_shape=(
            jax.ShapeDtypeStruct((slots * block_len, share), bf16),
            jax.ShapeDtypeStruct((slots, 2 * block_len, kv_width), bf16),
            jax.ShapeDtypeStruct((slots, 8, HEAD_SIZE), jnp.float32),
        ),
        in_specs=[vmem] * 5 + [smem] * 4 + [anywhere],
        out_specs=(anywhere,) * 3,
        scratch_shapes=[
            pltpu.VMEM((tps, depth, share), bf16),
            pltpu.VMEM((capacity, block_len, depth), bf16),
            pltpu.VMEM((groups, tps, rows, share), bf16),
            pltpu.VMEM((groups, tps + 1, rows, share), bf16),
            pltpu.VMEM((groups, rows, share), bf16),
            pltpu.VMEM((groups, capacity, 2 * block_len, kv_width), bf16),
            pltpu.VMEM((groups, capacity, 8, HEAD_SIZE), jnp.float32),
            dma((tps,)),
            dma((groups, tps)),
            dma((groups, tps + 1)),
            dma((groups,)), dma((groups,)),
            dma((groups,)), dma((groups,)),
            dma((groups,)), dma((groups,)),
            dma((3,)),
        ],
        compiler_params=pltpu.CompilerParams(
            collective_id=0, has_side_effects=True, vmem_limit_bytes=56 * 2**20
        ),
        cost_estimate=pl.CostEstimate(
            flops=2 * blocks * block_len * depth * (dout + 2 * 576),
            bytes_accessed=2 * depth * dout, transcendentals=0,
        ),
    )(
        queries.reshape(blocks, block_len, -1),
        keys.reshape(blocks, block_len, kv_width),
        values.reshape(blocks, block_len, kv_width),
        prefix_pool_keys, prefix_pool_values, lengths, targets, prefix_ids, owners, out_weight,
    )
    return (
        proj.reshape(slots, block_len, share),
        pages.reshape(slots, 2, block_len, kv_width),
        scales[:, :2, :kv_heads].astype(bf16),
    )


def solution(mesh):
    return jax.shard_map(
        on_device,
        mesh=mesh,
        in_specs=(
            P(("parts", "inst"), "tp"),
            P(("parts", "inst"), "tp"),
            P(("parts", "inst"), "tp"),
            P(("parts", "inst"), None, "tp"),
            P(("parts", "inst"), None, "tp"),
            P(("parts", "inst")),
            P(("parts", "inst"), None),
            P(("parts", "inst"), None),
            P(("parts", "inst"), None),
            P("tp", None),
        ),
        out_specs=(
            P(("parts", "inst"), None, "tp"),
            P(("parts", "inst"), None, None, "tp"),
            P(("parts", "inst"), None, "tp"),
        ),
        check_vma=False,
    )
```

```python
import functools
import math

import jax
import jax.numpy as jnp
from jax import lax
from jax.experimental import pallas as pl
from jax.experimental.pallas import tpu as pltpu
from jax.sharding import PartitionSpec as P

HEAD_SIZE = 128
MESH = pl.DeviceIdType.MESH
DEPTH = 2
PIECES = 4


def hadamard_table(size):
    row = lax.broadcasted_iota(jnp.int32, (size, size), 0)
    col = lax.broadcasted_iota(jnp.int32, (size, size), 1)
    common = jnp.bitwise_and(row, col)
    parity = jnp.zeros((size, size), jnp.int32)
    for bit_number in range(size.bit_length() - 1):
        parity = parity + jnp.bitwise_and(jnp.right_shift(common, bit_number), 1)
    return jnp.where(jnp.bitwise_and(parity, 1) == 0, 1.0, -1.0).astype(jnp.bfloat16)


def block_of(route_ref, blocks, group, rank):
    seen, found, valid = jnp.int32(0), jnp.int32(0), jnp.int32(0)
    for b in range(blocks):
        hit = (route_ref[b] == group).astype(jnp.int32)
        take = hit * (seen == rank).astype(jnp.int32)
        found = found + take * b
        valid = valid + take
        seen = seen + hit
    return found, valid


def attend(q_ref, k_ref, v_ref, pk_ref, pv_ref, ids_ref, block, length, attn_ref, row):
    block_len = q_ref.shape[1]
    kv_heads = k_ref.shape[2] // HEAD_SIZE
    group = q_ref.shape[2] // k_ref.shape[2]
    attended = ids_ref.shape[1]
    rate = math.log2(math.e) / math.sqrt(HEAD_SIZE)
    rows = group * block_len
    nt = (((1,), (1,)), ((), ()))
    token = lax.rem(lax.broadcasted_iota(jnp.int32, (rows, block_len), 0), block_len)
    place = lax.broadcasted_iota(jnp.int32, (rows, block_len), 1)
    allowed = (place <= token) & (place < length)
    live = lax.broadcasted_iota(jnp.int32, (block_len, HEAD_SIZE), 0) < length
    ids = [ids_ref[block, a] for a in range(attended)]
    for h in range(kv_heads):
        lanes = slice(h * HEAD_SIZE, (h + 1) * HEAD_SIZE)
        base = h * group * HEAD_SIZE
        q = jnp.concatenate(
            [q_ref[block, :, base + g * HEAD_SIZE : base + (g + 1) * HEAD_SIZE] for g in range(group)], axis=0
        )
        prefix_k = jnp.concatenate([pk_ref[i, :, lanes] for i in ids], axis=0)
        prefix_v = jnp.concatenate([pv_ref[i, :, lanes] for i in ids], axis=0)
        s0 = lax.dot_general(q, prefix_k, nt, preferred_element_type=jnp.float32)
        s1 = lax.dot_general(q, k_ref[block, :, lanes], nt, preferred_element_type=jnp.float32)
        s1 = jnp.where(allowed, s1, jnp.float32(-1e30))
        top = jnp.maximum(
            jnp.max(s0, axis=1, keepdims=True), jnp.max(s1, axis=1, keepdims=True)
        )
        p0 = jnp.exp2((s0 - top) * rate).astype(jnp.bfloat16)
        p1 = jnp.where(allowed, jnp.exp2((s1 - top) * rate), 0.0).astype(jnp.bfloat16)
        v0 = jnp.concatenate([prefix_v, jnp.ones_like(prefix_v)], axis=1)
        own_v = v_ref[block, :, lanes]
        v1 = jnp.concatenate([own_v, jnp.ones_like(own_v)], axis=1)
        mixed = jnp.dot(p0, v0, preferred_element_type=jnp.float32) + jnp.dot(
            p1, v1, preferred_element_type=jnp.float32
        )
        mixed = mixed[:, :HEAD_SIZE] / mixed[:, HEAD_SIZE:]
        for g in range(group):
            part = mixed[g * block_len : (g + 1) * block_len]
            attn_ref[row, :, base + g * HEAD_SIZE : base + (g + 1) * HEAD_SIZE] = jnp.where(
                live, part, 0.0
            ).astype(jnp.bfloat16)


def make_page(k_ref, v_ref, block, length, valid, table, page_ref, scale_ref, at, row):
    block_len = k_ref.shape[1]
    kv_heads = k_ref.shape[2] // HEAD_SIZE
    live = lax.broadcasted_iota(jnp.int32, (block_len, HEAD_SIZE), 0) < length
    tile_row = lax.broadcasted_iota(jnp.int32, (8, HEAD_SIZE), 0)
    tile = jnp.zeros((8, HEAD_SIZE), jnp.float32)
    for which, ref in enumerate((k_ref, v_ref)):
        for h in range(kv_heads):
            lanes = slice(h * HEAD_SIZE, (h + 1) * HEAD_SIZE)
            data = jnp.where(live, ref[block, :, lanes].astype(jnp.float32), 0.0).astype(jnp.bfloat16)
            rot = jnp.dot(data, table, preferred_element_type=jnp.float32) / math.sqrt(HEAD_SIZE)
            peak = jnp.max(jnp.max(jnp.abs(rot), axis=1, keepdims=True), axis=0, keepdims=True)
            scale = ((peak + 1e-06) / 8.0).astype(jnp.bfloat16).astype(jnp.float32)
            page_ref[at, row, which * block_len : (which + 1) * block_len, lanes] = (
                rot / scale
            ).astype(jnp.bfloat16)
            tile = jnp.where(tile_row == which * kv_heads + h, scale, tile)
    scale_ref[at, row] = tile * valid.astype(jnp.float32)


def kernel(
    groups, tps, capacity,
    q_ref, k_ref, v_ref, pk_ref, pv_ref, len_ref, tgt_ref, ids_ref, own_ref, w_ref,
    proj_ref, page_ref, scale_ref,
    w_buf, attn, send, recv, final, page_buf, scale_buf,
    w_sem, send_sem, recv_sem, ship_send, ship_recv, page_send, page_recv, scale_send, scale_recv, local_sem,
):
    part, inst, me = lax.axis_index("parts"), lax.axis_index("inst"), lax.axis_index("tp")
    blocks, block_len = q_ref.shape[0], q_ref.shape[1]
    share = w_buf.shape[2]
    last = tps - 1
    far = last - me

    def dest_at(p):
        right = p < far
        return jnp.where(right, last - p, jnp.where(p < last, p - far, me))

    def w_copy(p):
        j = dest_at(p)
        columns = pl.ds(pl.multiple_of(j * share, share), share)
        return pltpu.make_async_copy(w_ref.at[:, columns], w_buf.at[j], w_sem.at[p])

    for p in range(tps):
        w_copy(p).start()

    barrier = pltpu.get_barrier_semaphore()
    for d in range(1, groups):
        other = lax.rem(inst + d, groups)
        pl.semaphore_signal(barrier, inc=1, device_id=(part, other, me), device_id_type=MESH)

    @pl.when(me > 0)
    def _():
        pl.semaphore_signal(barrier, inc=1, device_id=(part, inst, me - 1), device_id_type=MESH)

    @pl.when(me < last)
    def _():
        pl.semaphore_signal(barrier, inc=1, device_id=(part, inst, me + 1), device_id_type=MESH)

    def target(i):
        return lax.rem(inst + 1 + i, groups)

    def source(i):
        return lax.rem(inst + groups - 1 - i, groups)

    table = hadamard_table(HEAD_SIZE)

    def page_step(n, carry):
        i, r = n // capacity, n % capacity
        b, valid = block_of(own_ref, blocks, target(i), r)
        length = len_ref[b] * valid
        make_page(k_ref, v_ref, b, length, valid, table, page_buf, scale_buf, i, r)
        return carry


    def page_copies(i, home):
        to = (part, target(i), me)
        slots = pl.ds(home * capacity, capacity)
        return (
            pltpu.make_async_remote_copy(
                src_ref=page_buf.at[i], dst_ref=page_ref.at[slots],
                send_sem=page_send.at[i], recv_sem=page_recv.at[i], device_id=to, device_id_type=MESH,
            ),
            pltpu.make_async_remote_copy(
                src_ref=scale_buf.at[i], dst_ref=scale_ref.at[slots],
                send_sem=scale_send.at[i], recv_sem=scale_recv.at[i], device_id=to, device_id_type=MESH,
            ),
        )

    def ship_copy(i, home):
        rows = pl.ds(pl.multiple_of(home * capacity * block_len, capacity * block_len), capacity * block_len)
        return pltpu.make_async_remote_copy(
            src_ref=final.at[i], dst_ref=proj_ref.at[rows],
            send_sem=ship_send.at[i], recv_sem=ship_recv.at[i],
            device_id=(part, target(i), me), device_id_type=MESH,
        )

    own = groups - 1
    own_slots = pl.ds(inst * capacity, capacity)
    own_rows = pl.ds(pl.multiple_of(inst * capacity * block_len, capacity * block_len), capacity * block_len)
    local_copies = (
        pltpu.make_async_copy(page_buf.at[own], page_ref.at[own_slots], local_sem.at[0]),
        pltpu.make_async_copy(scale_buf.at[own], scale_ref.at[own_slots], local_sem.at[1]),
        pltpu.make_async_copy(final.at[own], proj_ref.at[own_rows], local_sem.at[2]),
    )

    def send_pages():
        lax.fori_loop(0, groups * capacity, page_step, 0)
        for i in range(groups - 1):
            for copy in page_copies(i, inst):
                copy.start()
        local_copies[0].start()
        local_copies[1].start()

    def sum_copy(i, j):
        towards = jnp.where(j > me, me + 1, me - 1)
        slot = jnp.where((j < me) & (j == towards), tps, j)
        return pltpu.make_async_remote_copy(
            src_ref=send.at[i, j], dst_ref=recv.at[i, slot],
            send_sem=send_sem.at[i, j], recv_sem=recv_sem.at[i, slot],
            device_id=(part, inst, towards), device_id_type=MESH,
        )

    def arrived(i, slot):
        pltpu.make_async_copy(recv.at[i, slot], recv.at[i, slot], recv_sem.at[i, slot]).wait()

    def has_upstream(j):
        return ((j > me) & (me > 0)) | ((j < me) & (me < last))

    def compute(i):
        def one(r, carry):
            b, valid = block_of(tgt_ref, blocks, target(i), r)
            attend(q_ref, k_ref, v_ref, pk_ref, pv_ref, ids_ref, b, len_ref[b] * valid, attn, r)
            return carry

        lax.fori_loop(0, capacity, one, 0)

        @pl.when(i == 0)
        def _():
            neighbours = (me > 0).astype(jnp.int32) + (me < last).astype(jnp.int32)
            pl.semaphore_wait(barrier, groups - 1 + neighbours)

        wide = 256 if share % 256 == 0 else share

        def term(p, carry):
            j = dest_at(p)

            @pl.when(i == 0)
            def _():
                w_copy(p).wait()

            def columns(c, inner):
                lanes = pl.ds(pl.multiple_of(c * wide, wide), wide)
                rows = attn[...].reshape(capacity * block_len, attn.shape[2])
                send[i, j, :, lanes] = jnp.dot(
                    rows, w_buf[j, :, lanes], preferred_element_type=jnp.float32
                ).astype(jnp.bfloat16)
                return inner

            lax.fori_loop(0, share // wide, columns, 0)

            @pl.when((p < last) & jnp.logical_not(has_upstream(j)))
            def _():
                number = i * last + p

                @pl.when(number >= DEPTH)
                def _():
                    before = number - DEPTH
                    sum_copy(before // last, dest_at(before % last)).wait_send()

                sum_copy(i, j).start()

            return carry

        lax.fori_loop(0, tps, term, 0)

        @pl.when(i == 0)
        def _():
            send_pages()

    def forward(i):
        def one(p, carry):
            j = dest_at(p)

            @pl.when(has_upstream(j))
            def _():
                arrived(i, j)
                send[i, j] = (send[i, j].astype(jnp.float32) + recv[i, j].astype(jnp.float32)).astype(jnp.bfloat16)
                sum_copy(i, j).start()

            return carry

        lax.fori_loop(0, last, one, 0)

    def finish(i):
        final[i] = send[i, me]

        @pl.when((me > 0) & (me < last))
        def _():
            arrived(i, me)
            arrived(i, tps)
            final[i] = (
                send[i, me].astype(jnp.float32)
                + recv[i, me].astype(jnp.float32)
                + recv[i, tps].astype(jnp.float32)
            ).astype(jnp.bfloat16)

        @pl.when((me > 0) & (me == last))
        def _():
            arrived(i, me)
            final[i] = (send[i, me].astype(jnp.float32) + recv[i, me].astype(jnp.float32)).astype(jnp.bfloat16)

        @pl.when((me == 0) & (me < last))
        def _():
            arrived(i, tps)
            final[i] = (send[i, me].astype(jnp.float32) + recv[i, tps].astype(jnp.float32)).astype(jnp.bfloat16)

        @pl.when(i < own)
        def _():
            ship_copy(i, inst).start()

    def step(i, carry):
        @pl.when(i < groups)
        def _():
            compute(i)

        @pl.when(i > 0)
        def _():
            forward(i - 1)

        @pl.when(i > 1)
        def _():
            finish(i - 2)

        return carry

    lax.fori_loop(0, groups + 1, step, 0)
    finish(own)
    local_copies[2].start()

    def drain(i, carry):
        def one(p, inner):
            @pl.when(((me > 0) & (me < last)) | (i * last + p >= groups * last - DEPTH))
            def _():
                sum_copy(i, dest_at(p)).wait_send()

            return inner

        return lax.fori_loop(0, last, one, carry)

    lax.fori_loop(0, groups, drain, 0)
    for i in range(groups - 1):
        ship_copy(i, inst).wait_send()
        for copy in page_copies(i, inst):
            copy.wait_send()
        ship_copy(i, source(i)).wait_recv()
        for copy in page_copies(i, source(i)):
            copy.wait_recv()
    for copy in local_copies:
        copy.wait()


def deliver(proj_ref, page_ref, scale_ref, proj_out, page_out, scale_out):
    proj_out[...] = proj_ref[...]
    page_out[...] = page_ref[...]
    slots, kv_heads = scale_ref.shape[0], scale_out.shape[1]
    lane = lax.broadcasted_iota(jnp.int32, (8, HEAD_SIZE), 1)
    table = jnp.zeros((8, HEAD_SIZE), jnp.float32)
    for s in range(slots):
        table = jnp.where(lane == s, scale_ref[s], table)
    for which in range(2):
        scale_out[which] = table[which * kv_heads : (which + 1) * kv_heads, :slots].astype(scale_out.dtype)


def on_device(
    queries, keys, values, prefix_pool_keys, prefix_pool_values,
    lengths, targets, prefix_ids, owners, out_weight,
):
    groups, tps = lax.axis_size("inst"), lax.axis_size("tp")
    blocks, block_len = lengths.shape[0], prefix_pool_keys.shape[1]
    kv_width = keys.shape[1]
    kv_heads = kv_width // HEAD_SIZE
    capacity = max(1, (blocks + groups - 1) // groups)
    depth, dout = out_weight.shape
    share = dout // tps
    slots = groups * capacity
    rows = capacity * block_len
    vmem = pl.BlockSpec(memory_space=pltpu.VMEM)
    smem = pl.BlockSpec(memory_space=pltpu.SMEM)
    anywhere = pl.BlockSpec(memory_space=pl.ANY)
    dma = pltpu.SemaphoreType.DMA
    bf16 = jnp.bfloat16
    proj, pages, scales = pl.pallas_call(
        functools.partial(kernel, groups, tps, capacity),
        out_shape=(
            jax.ShapeDtypeStruct((slots * block_len, share), bf16),
            jax.ShapeDtypeStruct((slots, 2 * block_len, kv_width), bf16),
            jax.ShapeDtypeStruct((slots, 8, HEAD_SIZE), jnp.float32),
        ),
        in_specs=[vmem] * 5 + [smem] * 4 + [anywhere],
        out_specs=(anywhere,) * 3,
        scratch_shapes=[
            pltpu.VMEM((tps, depth, share), bf16),
            pltpu.VMEM((capacity, block_len, depth), bf16),
            pltpu.VMEM((groups, tps, rows, share), bf16),
            pltpu.VMEM((groups, tps + 1, rows, share), bf16),
            pltpu.VMEM((groups, rows, share), bf16),
            pltpu.VMEM((groups, capacity, 2 * block_len, kv_width), bf16),
            pltpu.VMEM((groups, capacity, 8, HEAD_SIZE), jnp.float32),
            dma((tps,)),
            dma((groups, tps)),
            dma((groups, tps + 1)),
            dma((groups,)), dma((groups,)),
            dma((groups,)), dma((groups,)),
            dma((groups,)), dma((groups,)),
            dma((3,)),
        ],
        compiler_params=pltpu.CompilerParams(
            collective_id=0, has_side_effects=True, vmem_limit_bytes=56 * 2**20
        ),
        cost_estimate=pl.CostEstimate(
            flops=2 * blocks * block_len * depth * (dout + 2 * 576),
            bytes_accessed=2 * depth * dout, transcendentals=0,
        ),
    )(
        queries.reshape(blocks, block_len, -1),
        keys.reshape(blocks, block_len, kv_width),
        values.reshape(blocks, block_len, kv_width),
        prefix_pool_keys, prefix_pool_values, lengths, targets.reshape(blocks), prefix_ids,
        owners.reshape(blocks), out_weight,
    )
    proj_spec = pl.BlockSpec((slots * block_len // PIECES, share), lambda n: (n, 0))
    page_spec = pl.BlockSpec((slots // PIECES, 2 * block_len, kv_width), lambda n: (n, 0, 0))
    scale_spec = pl.BlockSpec((slots, 8, HEAD_SIZE), lambda n: (0, 0, 0))
    table_spec = pl.BlockSpec((2, kv_heads, slots), lambda n: (0, 0, 0))
    proj, pages, scales = pl.pallas_call(
        deliver,
        out_shape=(
            jax.ShapeDtypeStruct(proj.shape, bf16),
            jax.ShapeDtypeStruct(pages.shape, bf16),
            jax.ShapeDtypeStruct((2, kv_heads, slots), bf16),
        ),
        grid=(PIECES,),
        in_specs=[proj_spec, page_spec, scale_spec],
        out_specs=(proj_spec, page_spec, table_spec),
    )(proj, pages, scales)
    return (
        proj.reshape(slots, block_len, share),
        pages.reshape(slots, 2, block_len, kv_width),
        scales.transpose(2, 0, 1),
    )


def solution(mesh):
    return jax.shard_map(
        on_device,
        mesh=mesh,
        in_specs=(
            P(("parts", "inst"), "tp"),
            P(("parts", "inst"), "tp"),
            P(("parts", "inst"), "tp"),
            P(("parts", "inst"), None, "tp"),
            P(("parts", "inst"), None, "tp"),
            P(("parts", "inst")),
            P(("parts", "inst"), None),
            P(("parts", "inst"), None),
            P(("parts", "inst"), None),
            P("tp", None),
        ),
        out_specs=(
            P(("parts", "inst"), None, "tp"),
            P(("parts", "inst"), None, None, "tp"),
            P(("parts", "inst"), None, "tp"),
        ),
        check_vma=False,
    )
```

```python
import functools
import math

import jax
import jax.numpy as jnp
from jax import lax
from jax.experimental import pallas as pl
from jax.experimental.pallas import tpu as pltpu
from jax.sharding import PartitionSpec as P

HEAD_SIZE = 128
MESH = pl.DeviceIdType.MESH
PIECES = 4


def hadamard_table(size):
    row = lax.broadcasted_iota(jnp.int32, (size, size), 0)
    col = lax.broadcasted_iota(jnp.int32, (size, size), 1)
    common = jnp.bitwise_and(row, col)
    parity = jnp.zeros((size, size), jnp.int32)
    for bit_number in range(size.bit_length() - 1):
        parity = parity + jnp.bitwise_and(jnp.right_shift(common, bit_number), 1)
    return jnp.where(jnp.bitwise_and(parity, 1) == 0, 1.0, -1.0).astype(jnp.bfloat16)


def block_of(route_ref, blocks, group, rank):
    seen, found, valid = jnp.int32(0), jnp.int32(0), jnp.int32(0)
    for b in range(blocks):
        hit = (route_ref[b] == group).astype(jnp.int32)
        take = hit * (seen == rank).astype(jnp.int32)
        found = found + take * b
        valid = valid + take
        seen = seen + hit
    return found, valid


def attend(q_ref, k_ref, v_ref, pk_ref, pv_ref, ids_ref, block, length, attn_ref, row):
    block_len = q_ref.shape[1]
    kv_heads = k_ref.shape[2] // HEAD_SIZE
    group = q_ref.shape[2] // k_ref.shape[2]
    attended = ids_ref.shape[1]
    rate = math.log2(math.e) / math.sqrt(HEAD_SIZE)
    rows = group * block_len
    nt = (((1,), (1,)), ((), ()))
    token = lax.rem(lax.broadcasted_iota(jnp.int32, (rows, block_len), 0), block_len)
    place = lax.broadcasted_iota(jnp.int32, (rows, block_len), 1)
    allowed = (place <= token) & (place < length)
    live = lax.broadcasted_iota(jnp.int32, (block_len, HEAD_SIZE), 0) < length
    ids = [ids_ref[block, a] for a in range(attended)]
    for h in range(kv_heads):
        lanes = slice(h * HEAD_SIZE, (h + 1) * HEAD_SIZE)
        base = h * group * HEAD_SIZE
        q = jnp.concatenate(
            [q_ref[block, :, base + g * HEAD_SIZE : base + (g + 1) * HEAD_SIZE] for g in range(group)], axis=0
        )
        prefix_k = jnp.concatenate([pk_ref[i, :, lanes] for i in ids], axis=0)
        prefix_v = jnp.concatenate([pv_ref[i, :, lanes] for i in ids], axis=0)
        s0 = lax.dot_general(q, prefix_k, nt, preferred_element_type=jnp.float32)
        s1 = lax.dot_general(q, k_ref[block, :, lanes], nt, preferred_element_type=jnp.float32)
        s1 = jnp.where(allowed, s1, jnp.float32(-1e30))
        top = jnp.maximum(
            jnp.max(s0, axis=1, keepdims=True), jnp.max(s1, axis=1, keepdims=True)
        )
        p0 = jnp.exp2((s0 - top) * rate).astype(jnp.bfloat16)
        p1 = jnp.where(allowed, jnp.exp2((s1 - top) * rate), 0.0).astype(jnp.bfloat16)
        v0 = jnp.concatenate([prefix_v, jnp.ones_like(prefix_v)], axis=1)
        own_v = v_ref[block, :, lanes]
        v1 = jnp.concatenate([own_v, jnp.ones_like(own_v)], axis=1)
        mixed = jnp.dot(p0, v0, preferred_element_type=jnp.float32) + jnp.dot(
            p1, v1, preferred_element_type=jnp.float32
        )
        mixed = mixed[:, :HEAD_SIZE] / mixed[:, HEAD_SIZE:]
        for g in range(group):
            part = mixed[g * block_len : (g + 1) * block_len]
            attn_ref[row, :, base + g * HEAD_SIZE : base + (g + 1) * HEAD_SIZE] = jnp.where(
                live, part, 0.0
            ).astype(jnp.bfloat16)


def make_page(k_ref, v_ref, block, length, valid, table, page_ref, scale_ref, at, row):
    block_len = k_ref.shape[1]
    kv_heads = k_ref.shape[2] // HEAD_SIZE
    live = lax.broadcasted_iota(jnp.int32, (block_len, HEAD_SIZE), 0) < length
    tile_row = lax.broadcasted_iota(jnp.int32, (8, HEAD_SIZE), 0)
    tile = jnp.zeros((8, HEAD_SIZE), jnp.float32)
    for which, ref in enumerate((k_ref, v_ref)):
        for h in range(kv_heads):
            lanes = slice(h * HEAD_SIZE, (h + 1) * HEAD_SIZE)
            data = jnp.where(live, ref[block, :, lanes].astype(jnp.float32), 0.0).astype(jnp.bfloat16)
            rot = jnp.dot(data, table, preferred_element_type=jnp.float32) / math.sqrt(HEAD_SIZE)
            peak = jnp.max(jnp.max(jnp.abs(rot), axis=1, keepdims=True), axis=0, keepdims=True)
            scale = ((peak + 1e-06) / 8.0).astype(jnp.bfloat16).astype(jnp.float32)
            page_ref[at, row, which * block_len : (which + 1) * block_len, lanes] = (
                rot / scale
            ).astype(jnp.bfloat16)
            tile = jnp.where(tile_row == which * kv_heads + h, scale, tile)
    scale_ref[at, row] = tile * valid.astype(jnp.float32)


def kernel(
    groups, tps, capacity,
    q_ref, k_ref, v_ref, pk_ref, pv_ref, len_ref, tgt_ref, ids_ref, own_ref, w_ref,
    proj_ref, page_ref, scale_ref,
    w_buf, attn, send, recv, final, page_buf, scale_buf,
    w_sem, send_sem, recv_sem, ship_send, ship_recv, page_send, page_recv, scale_send, scale_recv, local_sem,
):
    part, inst, me = lax.axis_index("parts"), lax.axis_index("inst"), lax.axis_index("tp")
    blocks, block_len = q_ref.shape[0], q_ref.shape[1]
    share = w_buf.shape[2]
    last = tps - 1
    far = last - me

    def dest_at(p):
        rightward = jnp.where(p < far, last - p, p - far)
        leftward = jnp.where(p < me, p, last - (p - me))
        return jnp.where(p < last, jnp.where(2 * me > last, leftward, rightward), me)

    def w_copy(p):
        j = dest_at(p)
        columns = pl.ds(pl.multiple_of(j * share, share), share)
        return pltpu.make_async_copy(w_ref.at[:, columns], w_buf.at[j], w_sem.at[p])

    for p in range(tps):
        w_copy(p).start()

    barrier = pltpu.get_barrier_semaphore()
    for d in range(1, groups):
        other = lax.rem(inst + d, groups)
        pl.semaphore_signal(barrier, inc=1, device_id=(part, other, me), device_id_type=MESH)

    @pl.when(me > 0)
    def _():
        pl.semaphore_signal(barrier, inc=1, device_id=(part, inst, me - 1), device_id_type=MESH)

    @pl.when(me < last)
    def _():
        pl.semaphore_signal(barrier, inc=1, device_id=(part, inst, me + 1), device_id_type=MESH)

    def target(i):
        return lax.rem(inst + 1 + i, groups)

    def source(i):
        return lax.rem(inst + groups - 1 - i, groups)

    table = hadamard_table(HEAD_SIZE)

    def page_step(n, carry):
        i, r = n // capacity, n % capacity
        b, valid = block_of(own_ref, blocks, target(i), r)
        length = len_ref[b] * valid
        make_page(k_ref, v_ref, b, length, valid, table, page_buf, scale_buf, i, r)
        return carry


    def page_copies(i, home):
        to = (part, target(i), me)
        slots = pl.ds(home * capacity, capacity)
        return (
            pltpu.make_async_remote_copy(
                src_ref=page_buf.at[i], dst_ref=page_ref.at[slots],
                send_sem=page_send.at[i], recv_sem=page_recv.at[i], device_id=to, device_id_type=MESH,
            ),
            pltpu.make_async_remote_copy(
                src_ref=scale_buf.at[i], dst_ref=scale_ref.at[slots],
                send_sem=scale_send.at[i], recv_sem=scale_recv.at[i], device_id=to, device_id_type=MESH,
            ),
        )

    def ship_copy(i, home):
        rows = pl.ds(pl.multiple_of(home * capacity * block_len, capacity * block_len), capacity * block_len)
        return pltpu.make_async_remote_copy(
            src_ref=final.at[i], dst_ref=proj_ref.at[rows],
            send_sem=ship_send.at[i], recv_sem=ship_recv.at[i],
            device_id=(part, target(i), me), device_id_type=MESH,
        )

    own = groups - 1
    own_slots = pl.ds(inst * capacity, capacity)
    own_rows = pl.ds(pl.multiple_of(inst * capacity * block_len, capacity * block_len), capacity * block_len)
    local_copies = (
        pltpu.make_async_copy(page_buf.at[own], page_ref.at[own_slots], local_sem.at[0]),
        pltpu.make_async_copy(scale_buf.at[own], scale_ref.at[own_slots], local_sem.at[1]),
        pltpu.make_async_copy(final.at[own], proj_ref.at[own_rows], local_sem.at[2]),
    )

    def send_pages():
        lax.fori_loop(0, groups * capacity, page_step, 0)
        for i in range(groups - 1):
            for copy in page_copies(i, inst):
                copy.start()
        local_copies[0].start()
        local_copies[1].start()

    def sum_copy(i, j):
        towards = jnp.where(j > me, me + 1, me - 1)
        slot = jnp.where((j < me) & (j == towards), tps, j)
        return pltpu.make_async_remote_copy(
            src_ref=send.at[i, j], dst_ref=recv.at[i, slot],
            send_sem=send_sem.at[i, j], recv_sem=recv_sem.at[i, slot],
            device_id=(part, inst, towards), device_id_type=MESH,
        )

    def arrived(i, slot):
        pltpu.make_async_copy(recv.at[i, slot], recv.at[i, slot], recv_sem.at[i, slot]).wait()

    def has_upstream(j):
        return ((j > me) & (me > 0)) | ((j < me) & (me < last))

    def compute(i):
        def one(r, carry):
            b, valid = block_of(tgt_ref, blocks, target(i), r)
            attend(q_ref, k_ref, v_ref, pk_ref, pv_ref, ids_ref, b, len_ref[b] * valid, attn, r)
            return carry

        lax.fori_loop(0, capacity, one, 0)

        @pl.when(i == 0)
        def _():
            neighbours = (me > 0).astype(jnp.int32) + (me < last).astype(jnp.int32)
            pl.semaphore_wait(barrier, groups - 1 + neighbours)

        wide = 256 if share % 256 == 0 else share

        def term(p, carry):
            j = dest_at(p)

            @pl.when(i == 0)
            def _():
                w_copy(p).wait()

            def columns(c, inner):
                lanes = pl.ds(pl.multiple_of(c * wide, wide), wide)
                rows = attn[...].reshape(capacity * block_len, attn.shape[2])
                send[i, j, :, lanes] = jnp.dot(
                    rows, w_buf[j, :, lanes], preferred_element_type=jnp.float32
                ).astype(jnp.bfloat16)
                return inner

            lax.fori_loop(0, share // wide, columns, 0)

            @pl.when((p < last) & jnp.logical_not(has_upstream(j)))
            def _():
                sum_copy(i, j).start()

            return carry

        lax.fori_loop(0, tps, term, 0)

        @pl.when(i == 0)
        def _():
            send_pages()

    def forward(i):
        def one(p, carry):
            j = dest_at(p)

            @pl.when(has_upstream(j))
            def _():
                arrived(i, j)
                send[i, j] = (send[i, j].astype(jnp.float32) + recv[i, j].astype(jnp.float32)).astype(jnp.bfloat16)
                sum_copy(i, j).start()

            return carry

        lax.fori_loop(0, last, one, 0)

    def finish(i):
        final[i] = send[i, me]

        @pl.when((me > 0) & (me < last))
        def _():
            arrived(i, me)
            arrived(i, tps)
            final[i] = (
                send[i, me].astype(jnp.float32)
                + recv[i, me].astype(jnp.float32)
                + recv[i, tps].astype(jnp.float32)
            ).astype(jnp.bfloat16)

        @pl.when((me > 0) & (me == last))
        def _():
            arrived(i, me)
            final[i] = (send[i, me].astype(jnp.float32) + recv[i, me].astype(jnp.float32)).astype(jnp.bfloat16)

        @pl.when((me == 0) & (me < last))
        def _():
            arrived(i, tps)
            final[i] = (send[i, me].astype(jnp.float32) + recv[i, tps].astype(jnp.float32)).astype(jnp.bfloat16)

        @pl.when(i < own)
        def _():
            ship_copy(i, inst).start()

    def step(i, carry):
        @pl.when(i < groups)
        def _():
            compute(i)

        @pl.when(i > 1)
        def _():
            finish(i - 2)

        @pl.when(i > 0)
        def _():
            forward(i - 1)

        return carry

    lax.fori_loop(0, groups + 1, step, 0)
    finish(own)
    local_copies[2].start()

    def drain(i, carry):
        def one(p, inner):
            sum_copy(i, dest_at(p)).wait_send()
            return inner

        return lax.fori_loop(0, last, one, carry)

    lax.fori_loop(0, groups, drain, 0)
    for i in range(groups - 1):
        ship_copy(i, inst).wait_send()
        for copy in page_copies(i, inst):
            copy.wait_send()
        ship_copy(i, source(i)).wait_recv()
        for copy in page_copies(i, source(i)):
            copy.wait_recv()
    for copy in local_copies:
        copy.wait()


def deliver(proj_ref, page_ref, scale_ref, proj_out, page_out, scale_out):
    proj_out[...] = proj_ref[...]
    page_out[...] = page_ref[...]
    slots, kv_heads = scale_ref.shape[0], scale_out.shape[1]
    lane = lax.broadcasted_iota(jnp.int32, (8, HEAD_SIZE), 1)
    table = jnp.zeros((8, HEAD_SIZE), jnp.float32)
    for s in range(slots):
        table = jnp.where(lane == s, scale_ref[s], table)
    for which in range(2):
        scale_out[which] = table[which * kv_heads : (which + 1) * kv_heads, :slots].astype(scale_out.dtype)


def on_device(
    queries, keys, values, prefix_pool_keys, prefix_pool_values,
    lengths, targets, prefix_ids, owners, out_weight,
):
    groups, tps = lax.axis_size("inst"), lax.axis_size("tp")
    blocks, block_len = lengths.shape[0], prefix_pool_keys.shape[1]
    kv_width = keys.shape[1]
    kv_heads = kv_width // HEAD_SIZE
    capacity = max(1, (blocks + groups - 1) // groups)
    depth, dout = out_weight.shape
    share = dout // tps
    slots = groups * capacity
    rows = capacity * block_len
    vmem = pl.BlockSpec(memory_space=pltpu.VMEM)
    smem = pl.BlockSpec(memory_space=pltpu.SMEM)
    anywhere = pl.BlockSpec(memory_space=pl.ANY)
    dma = pltpu.SemaphoreType.DMA
    bf16 = jnp.bfloat16
    proj, pages, scales = pl.pallas_call(
        functools.partial(kernel, groups, tps, capacity),
        out_shape=(
            jax.ShapeDtypeStruct((slots * block_len, share), bf16),
            jax.ShapeDtypeStruct((slots, 2 * block_len, kv_width), bf16),
            jax.ShapeDtypeStruct((slots, 8, HEAD_SIZE), jnp.float32),
        ),
        in_specs=[vmem] * 5 + [smem] * 4 + [anywhere],
        out_specs=(anywhere,) * 3,
        scratch_shapes=[
            pltpu.VMEM((tps, depth, share), bf16),
            pltpu.VMEM((capacity, block_len, depth), bf16),
            pltpu.VMEM((groups, tps, rows, share), bf16),
            pltpu.VMEM((groups, tps + 1, rows, share), bf16),
            pltpu.VMEM((groups, rows, share), bf16),
            pltpu.VMEM((groups, capacity, 2 * block_len, kv_width), bf16),
            pltpu.VMEM((groups, capacity, 8, HEAD_SIZE), jnp.float32),
            dma((tps,)),
            dma((groups, tps)),
            dma((groups, tps + 1)),
            dma((groups,)), dma((groups,)),
            dma((groups,)), dma((groups,)),
            dma((groups,)), dma((groups,)),
            dma((3,)),
        ],
        compiler_params=pltpu.CompilerParams(
            collective_id=0, has_side_effects=True, vmem_limit_bytes=56 * 2**20
        ),
        cost_estimate=pl.CostEstimate(
            flops=2 * blocks * block_len * depth * (dout + 2 * 576),
            bytes_accessed=2 * depth * dout, transcendentals=0,
        ),
    )(
        queries.reshape(blocks, block_len, -1),
        keys.reshape(blocks, block_len, kv_width),
        values.reshape(blocks, block_len, kv_width),
        prefix_pool_keys, prefix_pool_values, lengths, targets.reshape(blocks), prefix_ids,
        owners.reshape(blocks), out_weight,
    )
    proj_spec = pl.BlockSpec((slots * block_len // PIECES, share), lambda n: (n, 0))
    page_spec = pl.BlockSpec((slots // PIECES, 2 * block_len, kv_width), lambda n: (n, 0, 0))
    scale_spec = pl.BlockSpec((slots, 8, HEAD_SIZE), lambda n: (0, 0, 0))
    table_spec = pl.BlockSpec((2, kv_heads, slots), lambda n: (0, 0, 0))
    proj, pages, scales = pl.pallas_call(
        deliver,
        out_shape=(
            jax.ShapeDtypeStruct(proj.shape, bf16),
            jax.ShapeDtypeStruct(pages.shape, bf16),
            jax.ShapeDtypeStruct((2, kv_heads, slots), bf16),
        ),
        grid=(PIECES,),
        in_specs=[proj_spec, page_spec, scale_spec],
        out_specs=(proj_spec, page_spec, table_spec),
    )(proj, pages, scales)
    return (
        proj.reshape(slots, block_len, share),
        pages.reshape(slots, 2, block_len, kv_width),
        scales.transpose(2, 0, 1),
    )


def solution(mesh):
    return jax.shard_map(
        on_device,
        mesh=mesh,
        in_specs=(
            P(("parts", "inst"), "tp"),
            P(("parts", "inst"), "tp"),
            P(("parts", "inst"), "tp"),
            P(("parts", "inst"), None, "tp"),
            P(("parts", "inst"), None, "tp"),
            P(("parts", "inst")),
            P(("parts", "inst"), None),
            P(("parts", "inst"), None),
            P(("parts", "inst"), None),
            P("tp", None),
        ),
        out_specs=(
            P(("parts", "inst"), None, "tp"),
            P(("parts", "inst"), None, None, "tp"),
            P(("parts", "inst"), None, "tp"),
        ),
        check_vma=False,
    )
```
